128 devices in a mesh: win: 4 (over y_lo, core), chan: 32 (over x, y_hi, z).
Axes of the slice: x: 4, y: 4 (y_hi: 2, y_lo: 2; y = y_hi * 2 + y_lo), z: 4, core: 2. Of those that a mesh axis runs over, the one named last changes fastest.
Arguments:
- spectra: float32 [4, 2, 512, 8192], P('win', None, 'chan'), may hold values from -6 to 6
Outputs:
- stack: float32 [512, 64, 256], P('chan')
The draws below stay inside these ranges and needn't reach their ends.
All inputs are finite; a program needn't handle non-finite values.
Results may differ from the reference program's by a relative error of at most 0.000065.
Values sent between devices are 32-bit elements; how exact they have to be, the bound alone decides.
No kernel may reach another device: no remote copies, remote signals or barrier semaphores. Data moves between devices by JAX's collectives and lax.ppermute only.
A program may use at most 64 MiB of HBM per device.

```python
import math
import jax
import jax.numpy as jnp
from jax import lax

CH_DEV = 16
FREQS = 8192
LAGS = 256
STEPS = 4
WINDOWS = 4
CHANNELS = 512


def steps_of(own_key, extent, split, smallest, high):
    factor_of = 1.0
    for axis_at, shards_of in split:
        steps = jax.random.uniform(jax.random.fold_in(jax.random.fold_in(own_key, 6), axis_at), (shards_of,), jnp.float32, smallest / len(split), high / len(split))
        factor_of = factor_of * jnp.repeat(jnp.exp(steps), extent[axis_at] // shards_of).reshape((-1,) + (1,) * (len(extent) - 1 - axis_at))
    return factor_of


def normal_values(own_key, dims, scale, limit, cuts=(), dtype=jnp.bfloat16):
    gain = steps_of(own_key, dims, cuts, -0.22, 0.18) if cuts else 1.0
    values = jax.random.normal(own_key, dims, jnp.float32) * scale * gain
    return jnp.minimum(jnp.maximum(values, -limit), limit).astype(dtype)


def setup_inputs(seed: int = 0) -> dict:
    key_list = jax.random.split(jax.random.key(seed), 2)
    spectra = normal_values(key_list[0], (WINDOWS, 2, CHANNELS, FREQS), 1.0, 6.0, ((0, 4), (2, 32)), jnp.float32)
    return {"spectra": spectra}


def reference(spectra):
    stride = CHANNELS // STEPS
    pieces = [spectra[:, :, step * stride:step * stride + CH_DEV, :] for step in range(STEPS)]
    sources = jnp.concatenate(pieces, axis=2)
    ordered = jnp.moveaxis(sources, 2, 0)
    half_lags = LAGS // 2
    scale = math.sqrt(FREQS)
    real_part = spectra[:, 0]
    imag_part = spectra[:, 1]

    def per_source(source):
        src_real = source[:, 0][:, None, :]
        src_imag = source[:, 1][:, None, :]
        cross_real = real_part * src_real + imag_part * src_imag
        cross_imag = imag_part * src_real - real_part * src_imag
        inverse = jnp.fft.ifft(cross_real + 1j * cross_imag, axis=-1)
        values = jnp.real(inverse) * scale
        lagged = jnp.concatenate([values[..., FREQS - half_lags:], values[..., :half_lags]], axis=-1)
        return lax.optimization_barrier(jnp.sum(lagged, axis=0)) / WINDOWS
    result = lax.map(per_source, ordered)
    return jnp.transpose(result, (1, 0, 2)).astype(jnp.float32)
```

```python
import functools
import math

import jax
import jax.numpy as jnp
import numpy as np
from jax import lax
from jax.experimental import pallas as pl
from jax.experimental.pallas import tpu as pltpu
from jax.sharding import PartitionSpec as P

LAGS = 256
BINS = 8192
HALF = BINS // 2
CH = 16
WINDOWS = 4
PARTS = 8
W = HALF // PARTS
VMEM = pl.BlockSpec(memory_space=pltpu.VMEM)
SHIFTS = (1, -1, 2)


def tables():
    lag = np.arange(LAGS) - LAGS // 2
    turns = (np.arange(HALF)[:, None] * lag[None, :]) % BINS
    angle = 2.0 * np.pi * turns / BINS
    cosine, sine = np.cos(angle), -np.sin(angle)
    cosine[0], sine[0] = lag % 2 == 0, lag % 2 != 0
    table = np.concatenate([cosine.reshape(PARTS, W, LAGS), sine.reshape(PARTS, W, LAGS)], axis=1)
    table = table / (math.sqrt(BINS) * WINDOWS)
    high = table.astype(jnp.bfloat16)
    low = (table - high.astype(np.float64)).astype(jnp.bfloat16)
    return high, low


def fold_kernel(x_ref, all_ref, *quarter_refs):
    lane = lax.broadcasted_iota(jnp.int32, (8, 128), 1)
    mirror = lax.rem(128 - lane, 128)
    for part in range(2):
        for rows in (slice(0, 8), slice(8, 16)):
            for tile in range(HALF // 128):
                piece, offset = divmod(tile * 128, W)
                ahead = x_ref[part, rows, tile * 128 : tile * 128 + 128]
                last = BINS - tile * 128
                back = jnp.take_along_axis(x_ref[part, rows, last - 128 : last], mirror, axis=1)
                edge = last if tile else HALF
                back = jnp.where(lane == 0, x_ref[part, rows, edge : edge + 128] if edge < BINS else 0.0, back)
                columns = slice(offset, offset + 128)
                for row, value in ((part, ahead), (2 + part, back)):
                    all_ref[piece, row, rows, columns] = value
                    if piece >= 2:
                        quarter_refs[piece // 2 - 1][piece % 2, row, rows, columns] = value


def fold(x):
    shape = lambda n: jax.ShapeDtypeStruct((n, 4, CH, W), jnp.float32)
    return pl.pallas_call(
        fold_kernel,
        out_shape=[shape(PARTS)] + [shape(2)] * 3,
        in_specs=[VMEM],
        out_specs=[VMEM] * 4,
    )(x)


def correlate_kernel(ids, x_ref, a_ref, b0, b1, b2, b3, high_ref, low_ref, keep_ref, send_ref, y_ref, total, lh, ll):
    step = pl.program_id(0)
    piece = ids[step]

    @pl.when(step == 0)
    def _():
        total[...] = jnp.zeros_like(total)
        y_ref[0:4] = a_ref[...]
        for place, ref in enumerate((b0, b1, b2, b3)):
            y_ref[4 + place] = ref[...]

    y = [y_ref[step, k] for k in range(4)]
    first = jnp.logical_and(lax.broadcasted_iota(jnp.int32, (CH, 128), 1) == 0, piece == 0)
    for channel in range(CH):
        x = [x_ref[piece, k, channel : channel + 1, :] for k in range(4)]
        ahead = x[0] * y[0] + x[1] * y[1]
        back = x[2] * y[2] + x[3] * y[3]
        even = ahead + back
        odd = (x[1] * y[0] - x[0] * y[1]) + (x[2] * y[3] - x[3] * y[2])
        edge = jnp.where(first, ahead[:, :128] - back[:, :128], odd[:, :128])
        odd = jnp.concatenate([edge, odd[:, 128:]], axis=1)
        rows = slice(CH * channel, CH * channel + CH)
        for columns, value in ((slice(0, W), even), (slice(W, 2 * W), odd)):
            top = value.astype(jnp.bfloat16)
            lh[rows, columns] = top
            ll[rows, columns] = (value - top.astype(jnp.float32)).astype(jnp.bfloat16)
    dot = functools.partial(jnp.dot, preferred_element_type=jnp.float32)
    top, rest = lh[...], ll[...]
    got = dot(top, high_ref[0]) + dot(rest, high_ref[0]) + dot(top, low_ref[0])
    total[...] += got.reshape(CH, CH, LAGS)

    @pl.when(step == PARTS - 1)
    def _():
        core = ids[PARTS]
        keep_ref[...] = total[pl.ds(core * 8, 8)]
        send_ref[...] = total[pl.ds((1 - core) * 8, 8)]


def correlate(ids, x, a, b, high, low):
    whole = lambda *shape: pl.BlockSpec(shape, lambda i, ids: (0,) * len(shape))
    by_piece = pl.BlockSpec((1, 2 * W, LAGS), lambda i, ids: (ids[i], 0, 0))
    half = jax.ShapeDtypeStruct((CH // 2, CH, LAGS), jnp.float32)
    return pl.pallas_call(
        correlate_kernel,
        out_shape=[half, half],
        grid_spec=pltpu.PrefetchScalarGridSpec(
            num_scalar_prefetch=1,
            grid=(PARTS,),
            in_specs=[whole(PARTS, 4, CH, W), whole(4, 4, CH, W)] + [whole(4, CH, W)] * 4 + [by_piece] * 2,
            out_specs=[whole(CH // 2, CH, LAGS)] * 2,
            scratch_shapes=[
                pltpu.VMEM((PARTS, 4, CH, W), jnp.float32),
                pltpu.VMEM((CH, CH, LAGS), jnp.float32),
                pltpu.VMEM((CH * CH, 2 * W), jnp.bfloat16),
                pltpu.VMEM((CH * CH, 2 * W), jnp.bfloat16),
            ],
        ),
        compiler_params=pltpu.CompilerParams(vmem_limit_bytes=32 * 2**20),
        cost_estimate=pl.CostEstimate(
            flops=6 * CH * CH * 2 * HALF * LAGS, bytes_accessed=12 * 2**20, transcendentals=0
        ),
    )(ids, x, a, *b, high, low)


def place_kernel(where_ref, *refs):
    out_ref = refs[-1]
    core = where_ref[4]
    for block in range(4):
        at = where_ref[block]
        out_ref[pl.ds(core * 8, 8), at] = refs[2 * block][...]
        out_ref[pl.ds((1 - core) * 8, 8), at] = refs[2 * block + 1][...]


def place(where, pieces):
    return pl.pallas_call(
        place_kernel,
        out_shape=jax.ShapeDtypeStruct((CH, 4, CH, LAGS), jnp.float32),
        in_specs=[pl.BlockSpec(memory_space=pltpu.SMEM)] + [VMEM] * 8,
        out_specs=VMEM,
    )(where, *pieces)


def shards(spectra):
    me = lax.axis_index("chan")
    at_x, at_h, at_z = me // 8, me // 4 % 2, me % 4
    core = lax.axis_index("win") % 2
    along_x = lambda value, d: lax.ppermute(value, "chan", [(c, (c + 8 * d) % 32) for c in range(32)])
    along_z = lambda value, d: lax.ppermute(value, "chan", [(c, c // 4 * 4 + (c + d) % 4) for c in range(32)])
    other_core = lambda value: lax.ppermute(value, "win", [(w, w ^ 1) for w in range(4)])
    other_chip = lambda value: lax.ppermute(value, "win", [(w, w ^ 2) for w in range(4)])

    high, low = (jnp.asarray(t) for t in tables())
    x, *quarters = fold(spectra[0])
    got = [lax.ppermute(quarters[z - 1], "chan", [(8 * s, 8 * s + z) for s in range(4)]) for z in (1, 2, 3)]
    mine = jnp.where(at_z == 0, x[0:2], got[0] + got[1] + got[2])
    over = lax.ppermute(mine, "chan", [(8 * s + z, 8 * s + 4 + z) for s in range(4) for z in range(4)])
    mine = jnp.where(at_h == 0, mine, over)
    a, b = mine[0], mine[1]
    a_parts, b_blocks = [a], [b]
    for d in SHIFTS:
        a_parts.append(along_z(a, d))
        b_blocks.append(along_x(b, d))
    a_own = jnp.stack(a_parts)
    a_blocks = [a_own] + [along_x(a_own, d) for d in SHIFTS]
    b_parts = [[block] + [along_z(block, d) for d in SHIFTS] for block in b_blocks]

    back = jnp.array((0,) + SHIFTS, jnp.int32)
    from_z = (at_z - back) % 4
    ids = jnp.concatenate([2 * from_z, 2 * from_z + 1, core[None]]).astype(jnp.int32)
    placed = []
    for a_block, b_block in zip(a_blocks, b_parts):
        keep, send = correlate(ids, x, a_block, b_block, high, low)
        pair = keep + other_core(send)
        both = pair + other_chip(pair)
        placed += [both, other_core(both)]
    where = jnp.concatenate([(at_x - back) % 4, core[None]]).astype(jnp.int32)
    return place(where, placed).reshape(CH, 4 * CH, LAGS)


def solution(mesh):
    return jax.shard_map(
        shards,
        mesh=mesh,
        in_specs=(P("win", None, "chan", None),),
        out_specs=P("chan", None, None),
        check_vma=False,
    )
```

```python
import functools
import math

import jax
import jax.numpy as jnp
import numpy as np
from jax import lax
from jax.experimental import pallas as pl
from jax.experimental.pallas import tpu as pltpu
from jax.sharding import PartitionSpec as P

LAGS = 256
BINS = 8192
HALF = BINS // 2
CH = 16
WINDOWS = 4
PARTS = 8
W = HALF // PARTS
VMEM = pl.BlockSpec(memory_space=pltpu.VMEM)
SHIFTS = (1, -1, 2)


def tables():
    lag = np.arange(LAGS) - LAGS // 2
    turns = (np.arange(HALF)[:, None] * lag[None, :]) % BINS
    angle = 2.0 * np.pi * turns / BINS
    cosine, sine = np.cos(angle), -np.sin(angle)
    cosine[0], sine[0] = lag % 2 == 0, lag % 2 != 0
    table = np.concatenate([cosine.reshape(PARTS, W, LAGS), sine.reshape(PARTS, W, LAGS)], axis=1)
    table = table / (math.sqrt(BINS) * WINDOWS)
    high = table.astype(jnp.bfloat16)
    low = (table - high.astype(np.float64)).astype(jnp.bfloat16)
    return high, low


def fold_kernel(x_ref, all_ref, *quarter_refs):
    lane = lax.broadcasted_iota(jnp.int32, (8, 128), 1)
    mirror = lax.rem(128 - lane, 128)
    for part in range(2):
        for rows in (slice(0, 8), slice(8, 16)):
            for tile in range(HALF // 128):
                piece, offset = divmod(tile * 128, W)
                ahead = x_ref[part, rows, tile * 128 : tile * 128 + 128]
                last = BINS - tile * 128
                back = jnp.take_along_axis(x_ref[part, rows, last - 128 : last], mirror, axis=1)
                edge = last if tile else HALF
                back = jnp.where(lane == 0, x_ref[part, rows, edge : edge + 128] if edge < BINS else 0.0, back)
                columns = slice(offset, offset + 128)
                for row, value in ((part, ahead), (2 + part, back)):
                    all_ref[piece, row, rows, columns] = value
                    if piece >= 2:
                        quarter_refs[piece // 2 - 1][piece % 2, row, rows, columns] = value


def fold(x):
    shape = lambda n: jax.ShapeDtypeStruct((n, 4, CH, W), jnp.float32)
    return pl.pallas_call(
        fold_kernel,
        out_shape=[shape(PARTS)] + [shape(2)] * 3,
        in_specs=[VMEM],
        out_specs=[VMEM] * 4,
        compiler_params=pltpu.CompilerParams(vmem_limit_bytes=12 * 2**20),
    )(x)


def add_parts(ids, x_ref, g_ref, high_ref, low_ref, total, lh, ll):
    lane = lax.broadcasted_iota(jnp.int32, (CH, 128), 1)
    dot = functools.partial(jnp.dot, preferred_element_type=jnp.float32)
    for place in range(4):
        block, bins = ids[place], ids[4 + place]
        first = jnp.logical_and(lane == 0, bins == 0)
        for part in range(2):
            y = [g_ref[place, part, k] for k in range(4)]
            for channel in range(CH):
                x = [x_ref[2 * bins + part, k, channel : channel + 1, :] for k in range(4)]
                ahead = x[0] * y[0] + x[1] * y[1]
                back = x[2] * y[2] + x[3] * y[3]
                even = ahead + back
                odd = (x[1] * y[0] - x[0] * y[1]) + (x[2] * y[3] - x[3] * y[2])
                if part == 0:
                    edge = jnp.where(first, ahead[:, :128] - back[:, :128], odd[:, :128])
                    odd = jnp.concatenate([edge, odd[:, 128:]], axis=1)
                rows = slice(CH * channel, CH * channel + CH)
                for half, value in enumerate((even, odd)):
                    columns = slice((2 * part + half) * W, (2 * part + half + 1) * W)
                    top = value.astype(jnp.bfloat16)
                    lh[rows, columns] = top
                    ll[rows, columns] = (value - top.astype(jnp.float32)).astype(jnp.bfloat16)
        top, rest = lh[...], ll[...]
        high = high_ref[pl.ds(2 * bins, 2)].reshape(4 * W, LAGS)
        low = low_ref[pl.ds(2 * bins, 2)].reshape(4 * W, LAGS)
        got = dot(top, high) + dot(rest, high) + dot(top, low)
        total[block] += got.reshape(CH, CH, LAGS)


def first_kernel(ids, x_ref, g_ref, high_ref, low_ref, total, lh, ll):
    total[...] = jnp.zeros_like(total)
    add_parts(ids, x_ref, g_ref, high_ref, low_ref, total, lh, ll)


def middle_kernel(ids, x_ref, g_ref, high_ref, low_ref, before, total, lh, ll):
    add_parts(ids, x_ref, g_ref, high_ref, low_ref, total, lh, ll)


def last_kernel(ids, x_ref, g_ref, high_ref, low_ref, before, total, keep0, keep1, send0, send1, lh, ll):
    add_parts(ids, x_ref, g_ref, high_ref, low_ref, total, lh, ll)
    core = ids[8]
    for half, (keep, send) in enumerate(((keep0, send0), (keep1, send1))):
        keep[...] = total[2 * core + half]
        send[...] = total[2 * (1 - core) + half]


def correlate(kernel, ids, x, g, high, low, *total):
    here = lambda value: pltpu.with_memory_space_constraint(value, pltpu.VMEM)
    sums = jax.ShapeDtypeStruct((4, CH, CH, LAGS), jnp.float32)
    one = jax.ShapeDtypeStruct((CH, CH, LAGS), jnp.float32)
    outs = [sums] + ([one] * 4 if kernel is last_kernel else [])
    args = [here(value) for value in (x, g, high, low, *total)]
    return pl.pallas_call(
        kernel,
        out_shape=outs,
        in_specs=[pl.BlockSpec(memory_space=pltpu.SMEM)] + [VMEM] * len(args),
        out_specs=[VMEM] * len(outs),
        scratch_shapes=[pltpu.VMEM((CH * CH, 4 * W), jnp.bfloat16)] * 2,
        input_output_aliases={5: 0} if total else {},
        compiler_params=pltpu.CompilerParams(vmem_limit_bytes=16 * 2**20),
        cost_estimate=pl.CostEstimate(
            flops=6 * CH * CH * 2 * HALF * LAGS, bytes_accessed=12 * 2**20, transcendentals=0
        ),
    )(ids, *args)


def place_kernel(core_ref, *refs):
    out_ref = refs[-1]
    core = core_ref[0]
    for half in range(2):
        mine, other = refs[2 * half : 2 * half + 2]
        out_ref[:, 2 * core + half] = mine[...]
        out_ref[:, 2 * (1 - core) + half] = other[...]


def place(core, pieces):
    return pl.pallas_call(
        place_kernel,
        out_shape=jax.ShapeDtypeStruct((CH, 4, CH, LAGS), jnp.float32),
        in_specs=[pl.BlockSpec(memory_space=pltpu.SMEM)] + [VMEM] * len(pieces),
        out_specs=VMEM,
        compiler_params=pltpu.CompilerParams(vmem_limit_bytes=8 * 2**20),
    )(core, *pieces)


def stage_kernel(high_ref, low_ref, high_out, low_out, sems):
    copies = [
        pltpu.make_async_copy(source, target, sems.at[at])
        for at, (source, target) in enumerate(((high_ref, high_out), (low_ref, low_out)))
    ]
    for copy in copies:
        copy.start()
    for copy in copies:
        copy.wait()


def stage(high, low):
    return pl.pallas_call(
        stage_kernel,
        out_shape=[pltpu.VMEM(high.shape, high.dtype), pltpu.VMEM(low.shape, low.dtype)],
        in_specs=[pl.BlockSpec(memory_space=pl.ANY)] * 2,
        out_specs=[VMEM] * 2,
        scratch_shapes=[pltpu.SemaphoreType.DMA((2,))],
        compiler_params=pltpu.CompilerParams(vmem_limit_bytes=2**20),
    )(high, low)


def shards(spectra):
    me = lax.axis_index("chan")
    at_x, at_h, at_z = me // 8, me // 4 % 2, me % 4
    core = lax.axis_index("win") % 2
    over_x = lambda c, d: (c + 8 * d) % 32
    over_z = lambda c, d: c // 4 * 4 + (c + d) % 4

    def send(value, d, even, odd):
        pairs = [(w * 32 + c, w * 32 + (odd if w % 2 else even)(c, d)) for w in range(4) for c in range(32)]
        return lax.ppermute(value, ("win", "chan"), pairs)

    other_core = lambda value: lax.ppermute(value, "win", [(w, w ^ 1) for w in range(4)])
    other_chip = lambda value: lax.ppermute(value, "win", [(w, w ^ 2) for w in range(4)])

    high, low = stage(*(jnp.asarray(t) for t in tables()))
    x, *quarters = fold(spectra[0])
    got = [lax.ppermute(quarters[z - 1], "chan", [(8 * s, 8 * s + z) for s in range(4)]) for z in (1, 2, 3)]
    mine = jnp.where(at_z == 0, x[0:2], got[0] + got[1] + got[2])
    mine, high, low = lax.optimization_barrier((mine, high, low))
    over = lax.ppermute(mine, "chan", [(8 * s + z, 8 * s + 4 + z) for s in range(4) for z in range(4)])
    mine = jnp.where(at_h == 0, mine, over)
    group = jnp.stack([mine] + [send(mine, d, over_z, over_x) for d in SHIFTS])
    groups = [group] + [send(group, d, over_x, over_z) for d in SHIFTS]

    shifts = (0,) + SHIFTS
    kernels = [first_kernel, middle_kernel, middle_kernel, last_kernel]
    total = ()
    for kernel, shift, value in zip(kernels, shifts, groups):
        blocks = [jnp.where(core == 0, at_x - shift, at_x - d) % 4 for d in shifts]
        bins = [jnp.where(core == 0, at_z - d, at_z - shift) % 4 for d in shifts]
        ids = jnp.stack(blocks + bins + [core]).astype(jnp.int32)
        total = correlate(kernel, ids, x, value, high, low, *total)
        total, pieces = total[:1], total[1:]
    placed = []
    for keep, give in zip(pieces[:2], pieces[2:]):
        pair = keep + other_core(give)
        both = pair + other_chip(pair)
        placed += [both, other_core(both)]
    return place(core[None].astype(jnp.int32), placed).reshape(CH, 4 * CH, LAGS)


def solution(mesh):
    return jax.shard_map(
        shards,
        mesh=mesh,
        in_specs=(P("win", None, "chan", None),),
        out_specs=P("chan", None, None),
        check_vma=False,
    )
```

```python
import functools
import math

import jax
import jax.numpy as jnp
import numpy as np
from jax import lax
from jax.experimental import pallas as pl
from jax.experimental.pallas import tpu as pltpu
from jax.sharding import PartitionSpec as P

LAGS = 256
BINS = 8192
HALF = BINS // 2
CH = 16
WINDOWS = 4
PARTS = 8
W = HALF // PARTS
VMEM = pl.BlockSpec(memory_space=pltpu.VMEM)
HALVES = ((1, 3), (0, 2))


def tables():
    lag = np.arange(LAGS) - LAGS // 2
    turns = (np.arange(HALF)[:, None] * lag[None, :]) % BINS
    angle = 2.0 * np.pi * turns / BINS
    cosine, sine = np.cos(angle), -np.sin(angle)
    cosine[0], sine[0] = lag % 2 == 0, lag % 2 != 0
    table = np.concatenate([cosine.reshape(PARTS, W, LAGS), sine.reshape(PARTS, W, LAGS)], axis=1)
    table = table / (math.sqrt(BINS) * WINDOWS)
    high = table.astype(jnp.bfloat16)
    low = (table - high.astype(np.float64)).astype(jnp.bfloat16)
    return high, low


def fold_kernel(x_ref, all_ref, *quarter_refs):
    lane = lax.broadcasted_iota(jnp.int32, (8, 128), 1)
    mirror = lax.rem(128 - lane, 128)
    for part in range(2):
        for rows in (slice(0, 8), slice(8, 16)):
            for tile in range(HALF // 128):
                piece, offset = divmod(tile * 128, W)
                ahead = x_ref[part, rows, tile * 128 : tile * 128 + 128]
                last = BINS - tile * 128
                back = jnp.take_along_axis(x_ref[part, rows, last - 128 : last], mirror, axis=1)
                edge = last if tile else HALF
                back = jnp.where(lane == 0, x_ref[part, rows, edge : edge + 128] if edge < BINS else 0.0, back)
                columns = slice(offset, offset + 128)
                for row, value in ((part, ahead), (2 + part, back)):
                    all_ref[piece, row, rows, columns] = value
                    if piece >= 2:
                        quarter_refs[piece // 2 - 1][piece % 2, row, rows, columns] = value


def fold(x):
    shape = lambda n: jax.ShapeDtypeStruct((n, 4, CH, W), jnp.float32)
    return pl.pallas_call(
        fold_kernel,
        out_shape=[shape(PARTS)] + [shape(2)] * 3,
        in_specs=[VMEM],
        out_specs=[VMEM] * 4,
        compiler_params=pltpu.CompilerParams(vmem_limit_bytes=12 * 2**20),
    )(x)


def position():
    chan = lax.axis_index("chan")
    return chan // 8, chan % 4, lax.axis_index("win") % 2


def add_parts(sources, x_ref, high_ref, low_ref, total, lh, ll):
    at_x, at_z, core = position()
    lane = lax.broadcasted_iota(jnp.int32, (CH, 128), 1)
    dot = functools.partial(jnp.dot, preferred_element_type=jnp.float32)
    for g_ref, far, nears in sources:
        for place, near in enumerate(nears):
            block = (at_x + 4 - jnp.where(core == 0, far, near)) % 4
            bins = (at_z + 4 - jnp.where(core == 0, near, far)) % 4
            first = jnp.logical_and(lane == 0, bins == 0)
            for part in range(2):
                y = [g_ref[place, part, k] for k in range(4)]
                for channel in range(CH):
                    x = [x_ref[2 * bins + part, k, channel : channel + 1, :] for k in range(4)]
                    ahead = x[0] * y[0] + x[1] * y[1]
                    back = x[2] * y[2] + x[3] * y[3]
                    even = ahead + back
                    odd = (x[1] * y[0] - x[0] * y[1]) + (x[2] * y[3] - x[3] * y[2])
                    if part == 0:
                        edge = jnp.where(first, ahead[:, :128] - back[:, :128], odd[:, :128])
                        odd = jnp.concatenate([edge, odd[:, 128:]], axis=1)
                    rows = slice(CH * channel, CH * channel + CH)
                    for half, value in enumerate((even, odd)):
                        columns = slice((2 * part + half) * W, (2 * part + half + 1) * W)
                        top = value.astype(jnp.bfloat16)
                        lh[rows, columns] = top
                        ll[rows, columns] = (value - top.astype(jnp.float32)).astype(jnp.bfloat16)
            top = lh[...]
            high = high_ref[pl.ds(2 * bins, 2)].reshape(4 * W, LAGS)
            low = low_ref[pl.ds(2 * bins, 2)].reshape(4 * W, LAGS)
            both = dot(jnp.concatenate([top, ll[...]], axis=0), high)
            got = both[: CH * CH] + both[CH * CH :] + dot(top, low)
            total[block] += got.reshape(CH, CH, LAGS)


def correlate_kernel(steps, started, finished, x_ref, high_ref, low_ref, *refs):
    n = len(steps)
    total = refs[n + started]
    if not started:
        total[...] = jnp.zeros_like(total)
    sources = [(ref, far, nears) for ref, (far, nears) in zip(refs[:n], steps)]
    add_parts(sources, x_ref, high_ref, low_ref, total, *refs[-2:])
    if finished is not None:
        at_x, _, core = position()
        keep, send = refs[n + started + 1 : n + started + 3]
        here, there = finished
        keep[...] = total[(at_x + jnp.where(core == 0, here, there)) % 4]
        send[...] = total[(at_x + jnp.where(core == 0, there, here)) % 4]


def correlate(steps, values, tables, total=None, finished=None):
    here = lambda value: pltpu.with_memory_space_constraint(value, pltpu.VMEM)
    started = total is not None
    args = [here(value) for value in (*tables, *values, *([total] if started else []))]
    sums = jax.ShapeDtypeStruct((4, CH, CH, LAGS), jnp.float32)
    one = jax.ShapeDtypeStruct((CH, CH, LAGS), jnp.float32)
    outs = [sums] + ([one] * 2 if finished is not None else [])
    pairs = 2 * len(steps)
    return pl.pallas_call(
        functools.partial(correlate_kernel, steps, started, finished),
        out_shape=outs,
        in_specs=[VMEM] * len(args),
        out_specs=[VMEM] * len(outs),
        scratch_shapes=[pltpu.VMEM((CH * CH, 4 * W), jnp.bfloat16)] * 2,
        input_output_aliases={len(args) - 1: 0} if started else {},
        compiler_params=pltpu.CompilerParams(vmem_limit_bytes=16 * 2**20),
        cost_estimate=pl.CostEstimate(
            flops=6 * CH * CH * 4 * W * LAGS * pairs, bytes_accessed=3 * 2**20 * pairs, transcendentals=0
        ),
    )(*args)


def place_kernel(*refs):
    out_ref = refs[-1]
    at_x, _, core = position()
    for pair, (here, there) in enumerate(HALVES):
        mine, other = refs[2 * pair : 2 * pair + 2]
        out_ref[:, (at_x + jnp.where(core == 0, here, there)) % 4] = mine[...]
        out_ref[:, (at_x + jnp.where(core == 0, there, here)) % 4] = other[...]


def place(pieces):
    return pl.pallas_call(
        place_kernel,
        out_shape=jax.ShapeDtypeStruct((CH, 4, CH, LAGS), jnp.float32),
        in_specs=[VMEM] * len(pieces),
        out_specs=VMEM,
        compiler_params=pltpu.CompilerParams(vmem_limit_bytes=8 * 2**20),
    )(*pieces)


def stage_kernel(high_ref, low_ref, high_out, low_out, sems):
    copies = [
        pltpu.make_async_copy(source, target, sems.at[at])
        for at, (source, target) in enumerate(((high_ref, high_out), (low_ref, low_out)))
    ]
    for copy in copies:
        copy.start()
    for copy in copies:
        copy.wait()


def stage(high, low):
    return pl.pallas_call(
        stage_kernel,
        out_shape=[pltpu.VMEM(high.shape, high.dtype), pltpu.VMEM(low.shape, low.dtype)],
        in_specs=[pl.BlockSpec(memory_space=pl.ANY)] * 2,
        out_specs=[VMEM] * 2,
        scratch_shapes=[pltpu.SemaphoreType.DMA((2,))],
        compiler_params=pltpu.CompilerParams(vmem_limit_bytes=2**20),
    )(high, low)


def shards(spectra):
    me = lax.axis_index("chan")
    at_start, at_near = me % 4 == 0, me // 4 % 2 == 0
    spectra, at_start, at_near = lax.optimization_barrier((spectra, at_start, at_near))
    over_x = lambda c, d: (c + 8 * d) % 32
    over_z = lambda c, d: c // 4 * 4 + (c + d) % 4

    def send(value, d, even, odd):
        pairs = [(w * 32 + c, w * 32 + (odd if w % 2 else even)(c, d)) for w in range(4) for c in range(32)]
        return lax.ppermute(value, ("win", "chan"), pairs)

    other_core = lambda value: lax.ppermute(value, "win", [(w, w ^ 1) for w in range(4)])
    other_chip = lambda value: lax.ppermute(value, "win", [(w, w ^ 2) for w in range(4)])

    high, low = stage(*(jnp.asarray(t) for t in tables()))
    x, *quarters = fold(spectra[0])
    got = [lax.ppermute(quarters[z - 1], "chan", [(8 * s, 8 * s + z) for s in range(4)]) for z in (1, 2, 3)]
    mine = jnp.where(at_start, x[0:2], got[0] + got[1] + got[2])
    mine, high, low = lax.optimization_barrier((mine, high, low))
    over = lax.ppermute(mine, "chan", [(8 * s + z, 8 * s + 4 + z) for s in range(4) for z in range(4)])
    mine = jnp.where(at_near, mine, over)
    came = {d: send(mine, d, over_z, over_x) for d in (1, -1, 2)}
    first = jnp.stack([came[1], came[-1]])
    second = jnp.stack([mine, came[2]])
    firsts, seconds = {0: first}, {0: second}
    for group, value in ((firsts, first), (seconds, second)):
        for d in (1, -1):
            group[d] = send(value, d, over_x, over_z)
    firsts[2] = send(firsts[1], 1, over_x, over_z)
    seconds[2] = send(seconds[-1], -1, over_x, over_z)

    near, ends = (1, -1), (0, 2)
    tabled = (x, high, low)
    total = correlate([(0, near), (0, ends)], [firsts[0], seconds[0]], tabled)[0]
    total = correlate([(1, near), (-1, near)], [firsts[1], firsts[-1]], tabled, total)[0]
    total = correlate([(1, ends), (-1, ends)], [seconds[1], seconds[-1]], tabled, total)[0]
    total, *pieces = correlate([(2, near)], [firsts[2]], tabled, total, HALVES[0])
    total, *others = correlate([(2, ends)], [seconds[2]], tabled, total, HALVES[1])
    placed = []
    for keep, give in (pieces, others):
        pair = keep + other_core(give)
        both = pair + other_chip(pair)
        placed += [both, other_core(both)]
    return place(placed).reshape(CH, 4 * CH, LAGS)


def solution(mesh):
    return jax.shard_map(
        shards,
        mesh=mesh,
        in_specs=(P("win", None, "chan", None),),
        out_specs=P("chan", None, None),
        check_vma=False,
    )
```

```python
import functools
import math

import jax
import jax.numpy as jnp
import numpy as np
from jax import lax
from jax.experimental import pallas as pl
from jax.experimental.pallas import tpu as pltpu
from jax.sharding import PartitionSpec as P

LAGS = 256
BINS = 8192
HALF = BINS // 2
CH = 16
WINDOWS = 4
PARTS = 8
W = HALF // PARTS
VMEM = pl.BlockSpec(memory_space=pltpu.VMEM)
HALVES = ((1, 3), (0, 2))


def tables():
    lag = np.arange(LAGS) - LAGS // 2
    turns = (np.arange(HALF)[:, None] * lag[None, :]) % BINS
    angle = 2.0 * np.pi * turns / BINS
    cosine, sine = np.cos(angle), -np.sin(angle)
    cosine[0], sine[0] = lag % 2 == 0, lag % 2 != 0
    table = np.concatenate([cosine.reshape(PARTS, W, LAGS), sine.reshape(PARTS, W, LAGS)], axis=1)
    table = table / (math.sqrt(BINS) * WINDOWS)
    high = table.astype(jnp.bfloat16)
    low = (table - high.astype(np.float64)).astype(jnp.bfloat16)
    return high, low


def fold_kernel(x_ref, all_ref, *quarter_refs):
    lane = lax.broadcasted_iota(jnp.int32, (8, 128), 1)
    mirror = lax.rem(128 - lane, 128)
    for part in range(2):
        for rows in (slice(0, 8), slice(8, 16)):
            for tile in range(HALF // 128):
                piece, offset = divmod(tile * 128, W)
                ahead = x_ref[part, rows, tile * 128 : tile * 128 + 128]
                last = BINS - tile * 128
                back = jnp.take_along_axis(x_ref[part, rows, last - 128 : last], mirror, axis=1)
                edge = last if tile else HALF
                back = jnp.where(lane == 0, x_ref[part, rows, edge : edge + 128] if edge < BINS else 0.0, back)
                columns = slice(offset, offset + 128)
                for row, value in ((part, ahead), (2 + part, back)):
                    all_ref[piece, row, rows, columns] = value
                    if piece >= 2:
                        quarter_refs[piece // 2 - 1][piece % 2, row, rows, columns] = value


def fold(x):
    shape = lambda n: jax.ShapeDtypeStruct((n, 4, CH, W), jnp.float32)
    return pl.pallas_call(
        fold_kernel,
        out_shape=[shape(PARTS)] + [shape(2)] * 3,
        in_specs=[VMEM],
        out_specs=[VMEM] * 4,
        compiler_params=pltpu.CompilerParams(vmem_limit_bytes=12 * 2**20),
    )(x)


def position():
    chan = lax.axis_index("chan")
    return chan // 8, chan % 4, lax.axis_index("win") % 2


def add_parts(sources, x_ref, high_ref, low_ref, total, lh, ll):
    at_x, at_z, core = position()
    lane = lax.broadcasted_iota(jnp.int32, (CH, 128), 1)
    dot = functools.partial(jnp.dot, preferred_element_type=jnp.float32)
    for g_ref, far, nears in sources:
        for place, near in enumerate(nears):
            block = (at_x + 4 - jnp.where(core == 0, far, near)) % 4
            bins = (at_z + 4 - jnp.where(core == 0, near, far)) % 4
            first = jnp.logical_and(lane == 0, bins == 0)
            for part in range(2):
                y = [g_ref[place, part, k] for k in range(4)]
                for channel in range(CH):
                    x = [x_ref[2 * bins + part, k, channel : channel + 1, :] for k in range(4)]
                    ahead = x[0] * y[0] + x[1] * y[1]
                    back = x[2] * y[2] + x[3] * y[3]
                    even = ahead + back
                    odd = (x[1] * y[0] - x[0] * y[1]) + (x[2] * y[3] - x[3] * y[2])
                    if part == 0:
                        edge = jnp.where(first, ahead[:, :128] - back[:, :128], odd[:, :128])
                        odd = jnp.concatenate([edge, odd[:, 128:]], axis=1)
                    rows = slice(CH * channel, CH * channel + CH)
                    for half, value in enumerate((even, odd)):
                        columns = slice((2 * part + half) * W, (2 * part + half + 1) * W)
                        top = value.astype(jnp.bfloat16)
                        lh[rows, columns] = top
                        ll[rows, columns] = (value - top.astype(jnp.float32)).astype(jnp.bfloat16)
            top = lh[...]
            high = high_ref[pl.ds(2 * bins, 2)].reshape(4 * W, LAGS)
            low = low_ref[pl.ds(2 * bins, 2)].reshape(4 * W, LAGS)
            both = dot(jnp.concatenate([top, ll[...]], axis=0), high)
            got = both[: CH * CH] + both[CH * CH :] + dot(top, low)
            total[block] += got.reshape(CH, CH, LAGS)


def correlate_kernel(steps, started, finished, x_ref, high_ref, low_ref, *refs):
    n = len(steps)
    total = refs[n + started]
    if not started:
        total[...] = jnp.zeros_like(total)
    sources = [(ref, far, nears) for ref, (far, nears) in zip(refs[:n], steps)]
    add_parts(sources, x_ref, high_ref, low_ref, total, *refs[-2:])
    if finished is not None:
        at_x, _, core = position()
        keep, send = refs[n + started + 1 : n + started + 3]
        here, there = finished
        keep[...] = total[(at_x + jnp.where(core == 0, here, there)) % 4]
        send[...] = total[(at_x + jnp.where(core == 0, there, here)) % 4]


def correlate(steps, values, tables, total=None, finished=None):
    here = lambda value: pltpu.with_memory_space_constraint(value, pltpu.VMEM)
    started = total is not None
    values = [value.reshape(-1, 2, 4, CH, W) for value in values]
    args = [here(value) for value in (*tables, *values, *([total] if started else []))]
    sums = jax.ShapeDtypeStruct((4, CH, CH, LAGS), jnp.float32)
    one = jax.ShapeDtypeStruct((CH, CH, LAGS), jnp.float32)
    outs = [sums] + ([one] * 2 if finished is not None else [])
    pairs = sum(len(nears) for _, nears in steps)
    return pl.pallas_call(
        functools.partial(correlate_kernel, steps, started, finished),
        out_shape=outs,
        in_specs=[VMEM] * len(args),
        out_specs=[VMEM] * len(outs),
        scratch_shapes=[pltpu.VMEM((CH * CH, 4 * W), jnp.bfloat16)] * 2,
        input_output_aliases={len(args) - 1: 0} if started else {},
        compiler_params=pltpu.CompilerParams(vmem_limit_bytes=16 * 2**20),
        cost_estimate=pl.CostEstimate(
            flops=6 * CH * CH * 4 * W * LAGS * pairs, bytes_accessed=3 * 2**20 * pairs, transcendentals=0
        ),
    )(*args)


def place_kernel(*refs):
    out_ref = refs[-1]
    at_x, _, core = position()
    for pair, (here, there) in enumerate(HALVES):
        mine, other = refs[2 * pair : 2 * pair + 2]
        out_ref[:, (at_x + jnp.where(core == 0, here, there)) % 4] = mine[...]
        out_ref[:, (at_x + jnp.where(core == 0, there, here)) % 4] = other[...]


def place(pieces):
    return pl.pallas_call(
        place_kernel,
        out_shape=jax.ShapeDtypeStruct((CH, 4, CH, LAGS), jnp.float32),
        in_specs=[VMEM] * len(pieces),
        out_specs=VMEM,
        compiler_params=pltpu.CompilerParams(vmem_limit_bytes=8 * 2**20),
    )(*pieces)


def stage_kernel(high_ref, low_ref, high_out, low_out, sems):
    copies = [
        pltpu.make_async_copy(source, target, sems.at[at])
        for at, (source, target) in enumerate(((high_ref, high_out), (low_ref, low_out)))
    ]
    for copy in copies:
        copy.start()
    for copy in copies:
        copy.wait()


def stage(high, low):
    return pl.pallas_call(
        stage_kernel,
        out_shape=[pltpu.VMEM(high.shape, high.dtype), pltpu.VMEM(low.shape, low.dtype)],
        in_specs=[pl.BlockSpec(memory_space=pl.ANY)] * 2,
        out_specs=[VMEM] * 2,
        scratch_shapes=[pltpu.SemaphoreType.DMA((2,))],
        compiler_params=pltpu.CompilerParams(vmem_limit_bytes=2**20),
    )(high, low)


def shards(spectra):
    me = lax.axis_index("chan")
    at_start, at_near = me % 4 == 0, me // 4 % 2 == 0
    spectra, at_start, at_near = lax.optimization_barrier((spectra, at_start, at_near))
    over_x = lambda c, d: (c + 8 * d) % 32
    over_z = lambda c, d: c // 4 * 4 + (c + d) % 4

    def send(value, d, even, odd):
        pairs = [(w * 32 + c, w * 32 + (odd if w % 2 else even)(c, d)) for w in range(4) for c in range(32)]
        return lax.ppermute(value, ("win", "chan"), pairs)

    other_core = lambda value: lax.ppermute(value, "win", [(w, w ^ 1) for w in range(4)])
    other_chip = lambda value: lax.ppermute(value, "win", [(w, w ^ 2) for w in range(4)])

    high, low = stage(*(jnp.asarray(t) for t in tables()))
    x, *quarters = fold(spectra[0])
    got = [lax.ppermute(quarters[z - 1], "chan", [(8 * s, 8 * s + z) for s in range(4)]) for z in (1, 2, 3)]
    mine = jnp.where(at_start, x[0:2], got[0] + got[1] + got[2])
    mine, high, low = lax.optimization_barrier((mine, high, low))
    over = lax.ppermute(mine, "chan", [(8 * s + z, 8 * s + 4 + z) for s in range(4) for z in range(4)])
    mine = jnp.where(at_near, mine, over)
    came = {d: send(mine, d, over_z, over_x) for d in (1, -1, 2)}
    first = jnp.stack([came[1], came[-1]])
    second = jnp.stack([mine, came[2]])
    firsts, seconds = {0: first}, {0: second}
    for group, value in ((firsts, first), (seconds, second)):
        for d in (1, -1):
            group[d] = send(value, d, over_x, over_z)
    firsts[2] = send(firsts[1], 1, over_x, over_z)
    seconds[2] = send(seconds[-1], -1, over_x, over_z)

    near, ends = (1, -1), (0, 2)
    tabled = (x, high, low)
    total = correlate([(0, near), (0, ends)], [firsts[0], seconds[0]], tabled)[0]
    total = correlate([(1, near), (-1, ends)], [firsts[1], seconds[-1]], tabled, total)[0]
    total = correlate([(-1, near), (1, ends)], [firsts[-1], seconds[1]], tabled, total)[0]
    total, keep, give = correlate([(2, near)], [firsts[2]], tabled, total, HALVES[0])
    pair = keep + other_core(give)
    total = correlate([(2, (0,))], [seconds[2][0]], tabled, total)[0]
    total, pair = lax.optimization_barrier((total, pair))
    both = pair + other_chip(pair)
    placed = [both, other_core(both)]
    _, keep, give = correlate([(2, (2,))], [seconds[2][1]], tabled, total, HALVES[1])
    pair = keep + other_core(give)
    both = pair + other_chip(pair)
    placed += [both, other_core(both)]
    return place(placed).reshape(CH, 4 * CH, LAGS)


def solution(mesh):
    return jax.shard_map(
        shards,
        mesh=mesh,
        in_specs=(P("win", None, "chan", None),),
        out_specs=P("chan", None, None),
        check_vma=False,
    )
```

```python
import functools
import math

import jax
import jax.numpy as jnp
import numpy as np
from jax import lax
from jax.experimental import pallas as pl
from jax.experimental.pallas import tpu as pltpu
from jax.sharding import PartitionSpec as P

LAGS = 256
BINS = 8192
HALF = BINS // 2
CH = 16
WINDOWS = 4
PARTS = 8
W = HALF // PARTS
VMEM = pl.BlockSpec(memory_space=pltpu.VMEM)
GROUPS = ((0, 1, 3), (2,))


def tables():
    lag = np.arange(LAGS) - LAGS // 2
    turns = (np.arange(HALF)[:, None] * lag[None, :]) % BINS
    angle = 2.0 * np.pi * turns / BINS
    cosine, sine = np.cos(angle), -np.sin(angle)
    cosine[0], sine[0] = lag % 2 == 0, lag % 2 != 0
    table = np.concatenate([cosine.reshape(PARTS, W, LAGS), sine.reshape(PARTS, W, LAGS)], axis=1)
    table = table / (math.sqrt(BINS) * WINDOWS)
    high = table.astype(jnp.bfloat16)
    low = (table - high.astype(np.float64)).astype(jnp.bfloat16)
    return high, low


def fold_kernel(x_ref, all_ref, *quarter_refs):
    lane = lax.broadcasted_iota(jnp.int32, (8, 128), 1)
    mirror = lax.rem(128 - lane, 128)
    for part in range(2):
        for rows in (slice(0, 8), slice(8, 16)):
            for tile in range(HALF // 128):
                piece, offset = divmod(tile * 128, W)
                ahead = x_ref[part, rows, tile * 128 : tile * 128 + 128]
                last = BINS - tile * 128
                back = jnp.take_along_axis(x_ref[part, rows, last - 128 : last], mirror, axis=1)
                edge = last if tile else HALF
                back = jnp.where(lane == 0, x_ref[part, rows, edge : edge + 128] if edge < BINS else 0.0, back)
                columns = slice(offset, offset + 128)
                for row, value in ((part, ahead), (2 + part, back)):
                    all_ref[piece, row, rows, columns] = value
                    if piece >= 2:
                        quarter_refs[piece // 2 - 1][piece % 2, row, rows, columns] = value


def fold(x):
    shape = lambda n: jax.ShapeDtypeStruct((n, 4, CH, W), jnp.float32)
    return pl.pallas_call(
        fold_kernel,
        out_shape=[shape(PARTS)] + [shape(2)] * 3,
        in_specs=[VMEM],
        out_specs=[VMEM] * 4,
        compiler_params=pltpu.CompilerParams(vmem_limit_bytes=12 * 2**20),
    )(x)


def position():
    chan = lax.axis_index("chan")
    return chan // 8, chan % 4, lax.axis_index("win") % 2


def add_parts(sources, x_ref, high_ref, low_ref, total, lh, ll):
    at_x, at_z, core = position()
    lane = lax.broadcasted_iota(jnp.int32, (CH, 128), 1)
    dot = functools.partial(jnp.dot, preferred_element_type=jnp.float32)
    for g_ref, far, nears, only in sources:

        def add(g_ref=g_ref, far=far, nears=nears):
            for place, near in enumerate(nears):
                block = (at_x + 4 - jnp.where(core == 0, far, near)) % 4
                bins = (at_z + 4 - jnp.where(core == 0, near, far)) % 4
                first = jnp.logical_and(lane == 0, bins == 0)
                for part in range(2):
                    y = [g_ref[place, part, k] for k in range(4)]
                    for channel in range(CH):
                        x = [x_ref[2 * bins + part, k, channel : channel + 1, :] for k in range(4)]
                        ahead = x[0] * y[0] + x[1] * y[1]
                        back = x[2] * y[2] + x[3] * y[3]
                        even = ahead + back
                        odd = (x[1] * y[0] - x[0] * y[1]) + (x[2] * y[3] - x[3] * y[2])
                        if part == 0:
                            edge = jnp.where(first, ahead[:, :128] - back[:, :128], odd[:, :128])
                            odd = jnp.concatenate([edge, odd[:, 128:]], axis=1)
                        rows = slice(CH * channel, CH * channel + CH)
                        for half, value in enumerate((even, odd)):
                            columns = slice((2 * part + half) * W, (2 * part + half + 1) * W)
                            top = value.astype(jnp.bfloat16)
                            lh[rows, columns] = top
                            ll[rows, columns] = (value - top.astype(jnp.float32)).astype(jnp.bfloat16)
                top = lh[...]
                high = high_ref[pl.ds(2 * bins, 2)].reshape(4 * W, LAGS)
                low = low_ref[pl.ds(2 * bins, 2)].reshape(4 * W, LAGS)
                both = dot(jnp.concatenate([top, ll[...]], axis=0), high)
                got = both[: CH * CH] + both[CH * CH :] + dot(top, low)
                total[block] += got.reshape(CH, CH, LAGS)

        if only is None:
            add()
        else:
            pl.when(core == only)(add)


def correlate_kernel(steps, started, finished, x_ref, high_ref, low_ref, *refs):
    n = len(steps)
    total = refs[n + started]
    if not started:
        total[...] = jnp.zeros_like(total)
    sources = [(ref, far, nears, *(only or [None])) for ref, (far, nears, *only) in zip(refs[:n], steps)]
    add_parts(sources, x_ref, high_ref, low_ref, total, *refs[-2:])
    if finished is not None:
        at_x, _, core = position()
        keep, send = refs[n + started + 1 : n + started + 3]
        for place, block in enumerate(finished):
            keep[place] = total[(at_x + block) % 4, pl.ds(8 * core, 8)]
            send[place] = total[(at_x + block) % 4, pl.ds(8 * (1 - core), 8)]


def correlate(steps, values, tables, total=None, finished=None):
    here = lambda value: pltpu.with_memory_space_constraint(value, pltpu.VMEM)
    started = total is not None
    values = [value.reshape(-1, 2, 4, CH, W) for value in values]
    args = [here(value) for value in (*tables, *values, *([total] if started else []))]
    sums = jax.ShapeDtypeStruct((4, CH, CH, LAGS), jnp.float32)
    half = lambda blocks: jax.ShapeDtypeStruct((len(blocks), 8, CH, LAGS), jnp.float32)
    outs = [sums] + ([half(finished)] * 2 if finished is not None else [])
    pairs = sum(len(step[1]) for step in steps)
    return pl.pallas_call(
        functools.partial(correlate_kernel, steps, started, finished),
        out_shape=outs,
        in_specs=[VMEM] * len(args),
        out_specs=[VMEM] * len(outs),
        scratch_shapes=[pltpu.VMEM((CH * CH, 4 * W), jnp.bfloat16)] * 2,
        input_output_aliases={len(args) - 1: 0} if started else {},
        compiler_params=pltpu.CompilerParams(vmem_limit_bytes=16 * 2**20),
        cost_estimate=pl.CostEstimate(
            flops=6 * CH * CH * 4 * W * LAGS * pairs, bytes_accessed=3 * 2**20 * pairs, transcendentals=0
        ),
    )(*args)


def place_kernel(*refs):
    out_ref = refs[-1]
    at_x, _, core = position()
    for pair, blocks in enumerate(GROUPS):
        mine, other = refs[2 * pair : 2 * pair + 2]
        for place, block in enumerate(blocks):
            out_ref[pl.ds(8 * core, 8), (at_x + block) % 4] = mine[place]
            out_ref[pl.ds(8 * (1 - core), 8), (at_x + block) % 4] = other[place]


def place(pieces):
    return pl.pallas_call(
        place_kernel,
        out_shape=jax.ShapeDtypeStruct((CH, 4, CH, LAGS), jnp.float32),
        in_specs=[VMEM] * len(pieces),
        out_specs=VMEM,
        compiler_params=pltpu.CompilerParams(vmem_limit_bytes=8 * 2**20),
    )(*pieces)


def stage_kernel(high_ref, low_ref, high_out, low_out, sems):
    copies = [
        pltpu.make_async_copy(source, target, sems.at[at])
        for at, (source, target) in enumerate(((high_ref, high_out), (low_ref, low_out)))
    ]
    for copy in copies:
        copy.start()
    for copy in copies:
        copy.wait()


def stage(high, low):
    return pl.pallas_call(
        stage_kernel,
        out_shape=[pltpu.VMEM(high.shape, high.dtype), pltpu.VMEM(low.shape, low.dtype)],
        in_specs=[pl.BlockSpec(memory_space=pl.ANY)] * 2,
        out_specs=[VMEM] * 2,
        scratch_shapes=[pltpu.SemaphoreType.DMA((2,))],
        compiler_params=pltpu.CompilerParams(vmem_limit_bytes=2**20),
    )(high, low)


def shards(spectra):
    me = lax.axis_index("chan")
    at_start, at_near = me % 4 == 0, me // 4 % 2 == 0
    spectra, at_start, at_near = lax.optimization_barrier((spectra, at_start, at_near))
    over_x = lambda c, d: (c + 8 * d) % 32
    over_z = lambda c, d: c // 4 * 4 + (c + d) % 4

    def send(value, d, even, odd):
        pairs = [(w * 32 + c, w * 32 + (odd if w % 2 else even)(c, d)) for w in range(4) for c in range(32)]
        return lax.ppermute(value, ("win", "chan"), pairs)

    other_core = lambda value: lax.ppermute(value, "win", [(w, w ^ 1) for w in range(4)])
    other_chip = lambda value: lax.ppermute(value, "win", [(w, w ^ 2) for w in range(4)])

    high, low = stage(*(jnp.asarray(t) for t in tables()))
    x, *quarters = fold(spectra[0])
    got = [lax.ppermute(quarters[z - 1], "chan", [(8 * s, 8 * s + z) for s in range(4)]) for z in (1, 2, 3)]
    mine = jnp.where(at_start, x[0:2], got[0] + got[1] + got[2])
    mine, high, low = lax.optimization_barrier((mine, high, low))
    over = lax.ppermute(mine, "chan", [(8 * s + z, 8 * s + 4 + z) for s in range(4) for z in range(4)])
    mine = jnp.where(at_near, mine, over)
    came = {d: send(mine, d, over_z, over_x) for d in (1, -1, 2)}
    first = jnp.stack([came[1], came[-1]])
    second = jnp.stack([mine, came[2]])
    firsts, seconds = {0: first}, {0: second}
    for group, value in ((firsts, first), (seconds, second)):
        for d in (1, -1):
            group[d] = send(value, d, over_x, over_z)
    firsts[2] = send(firsts[1], 1, over_x, over_z)
    seconds[2] = send(seconds[-1], -1, over_x, over_z)

    near, ends = (1, -1), (0, 2)
    tabled = (x, high, low)
    total = correlate([(0, near), (0, ends)], [firsts[0], seconds[0]], tabled)[0]
    total = correlate([(1, near), (-1, ends)], [firsts[1], seconds[-1]], tabled, total)[0]
    total = correlate([(-1, near), (1, ends)], [firsts[-1], seconds[1]], tabled, total)[0]
    values = [firsts[2], seconds[2][0]]
    total, keep, give = correlate([(2, near, 1), (2, (0,), 1)], values, tabled, total, GROUPS[0])
    pair = keep + other_core(give)
    total = correlate([(2, near, 0)], [firsts[2]], tabled, total)[0]
    total, pair = lax.optimization_barrier((total, pair))
    far_pair = other_chip(pair)
    values = [seconds[2][0], seconds[2][1]]
    _, keep, give = correlate([(2, (0,), 0), (2, (2,))], values, tabled, total, GROUPS[1])
    last = keep + other_core(give)
    far_last = other_chip(last)
    far_pair, far_last = lax.optimization_barrier((far_pair, far_last))
    both, both_last = pair + far_pair, last + far_last
    placed = [both, other_core(both), both_last, other_core(both_last)]
    return place(placed).reshape(CH, 4 * CH, LAGS)


def solution(mesh):
    return jax.shard_map(
        shards,
        mesh=mesh,
        in_specs=(P("win", None, "chan", None),),
        out_specs=P("chan", None, None),
        check_vma=False,
    )
```

```python
import functools
import math

import jax
import jax.numpy as jnp
import numpy as np
from jax import lax
from jax.experimental import pallas as pl
from jax.experimental.pallas import tpu as pltpu
from jax.sharding import PartitionSpec as P

LAGS = 256
BINS = 8192
HALF = BINS // 2
CH = 16
WINDOWS = 4
PARTS = 8
W = HALF // PARTS
VMEM = pl.BlockSpec(memory_space=pltpu.VMEM)
GROUPS = ((0, 1, 3), (2,))


def tables():
    lag = np.arange(LAGS) - LAGS // 2
    turns = (np.arange(HALF)[:, None] * lag[None, :]) % BINS
    angle = 2.0 * np.pi * turns / BINS
    cosine, sine = np.cos(angle), -np.sin(angle)
    cosine[0], sine[0] = lag % 2 == 0, lag % 2 != 0
    table = np.concatenate([cosine.reshape(PARTS, W, LAGS), sine.reshape(PARTS, W, LAGS)], axis=1)
    table = table / (math.sqrt(BINS) * WINDOWS)
    high = table.astype(jnp.bfloat16)
    low = (table - high.astype(np.float64)).astype(jnp.bfloat16)
    return high, low


def fold_kernel(x_ref, all_ref, *quarter_refs):
    lane = lax.broadcasted_iota(jnp.int32, (8, 128), 1)
    mirror = lax.rem(128 - lane, 128)
    for part in range(2):
        for rows in (slice(0, 8), slice(8, 16)):
            for tile in range(HALF // 128):
                piece, offset = divmod(tile * 128, W)
                ahead = x_ref[part, rows, tile * 128 : tile * 128 + 128]
                last = BINS - tile * 128
                back = jnp.take_along_axis(x_ref[part, rows, last - 128 : last], mirror, axis=1)
                edge = last if tile else HALF
                back = jnp.where(lane == 0, x_ref[part, rows, edge : edge + 128] if edge < BINS else 0.0, back)
                columns = slice(offset, offset + 128)
                for row, value in ((part, ahead), (2 + part, back)):
                    all_ref[piece, row, rows, columns] = value
                    if piece >= 2:
                        quarter_refs[piece // 2 - 1][piece % 2, row, rows, columns] = value


def fold(x):
    shape = lambda n: jax.ShapeDtypeStruct((n, 4, CH, W), jnp.float32)
    return pl.pallas_call(
        fold_kernel,
        out_shape=[shape(PARTS)] + [shape(2)] * 3,
        in_specs=[VMEM],
        out_specs=[VMEM] * 4,
        compiler_params=pltpu.CompilerParams(vmem_limit_bytes=12 * 2**20),
    )(x)


def position():
    chan = lax.axis_index("chan")
    return chan // 8, chan % 4, lax.axis_index("win") % 2


def add_parts(sources, x_ref, high_ref, low_ref, total, lh, ll):
    at_x, at_z, core = position()
    lane = lax.broadcasted_iota(jnp.int32, (CH, 128), 1)
    dot = functools.partial(jnp.dot, preferred_element_type=jnp.float32)
    for g_ref, far, nears, only in sources:

        def add(g_ref=g_ref, far=far, nears=nears):
            for place, near in enumerate(nears):
                near = jnp.where(jnp.where(core == 0, at_z, at_x) % 2 == 0, -near, near)
                block = (at_x + 4 - jnp.where(core == 0, far, near)) % 4
                bins = (at_z + 4 - jnp.where(core == 0, near, far)) % 4
                first = jnp.logical_and(lane == 0, bins == 0)
                for part in range(2):
                    y = [g_ref[place, part, k] for k in range(4)]
                    for channel in range(CH):
                        x = [x_ref[2 * bins + part, k, channel : channel + 1, :] for k in range(4)]
                        ahead = x[0] * y[0] + x[1] * y[1]
                        back = x[2] * y[2] + x[3] * y[3]
                        even = ahead + back
                        odd = (x[1] * y[0] - x[0] * y[1]) + (x[2] * y[3] - x[3] * y[2])
                        if part == 0:
                            edge = jnp.where(first, ahead[:, :128] - back[:, :128], odd[:, :128])
                            odd = jnp.concatenate([edge, odd[:, 128:]], axis=1)
                        rows = slice(CH * channel, CH * channel + CH)
                        for half, value in enumerate((even, odd)):
                            columns = slice((2 * part + half) * W, (2 * part + half + 1) * W)
                            top = value.astype(jnp.bfloat16)
                            lh[rows, columns] = top
                            ll[rows, columns] = (value - top.astype(jnp.float32)).astype(jnp.bfloat16)
                top = lh[...]
                high = high_ref[pl.ds(2 * bins, 2)].reshape(4 * W, LAGS)
                low = low_ref[pl.ds(2 * bins, 2)].reshape(4 * W, LAGS)
                both = dot(jnp.concatenate([top, ll[...]], axis=0), high)
                got = both[: CH * CH] + both[CH * CH :] + dot(top, low)
                total[block] += got.reshape(CH, CH, LAGS)

        if only is None:
            add()
        else:
            pl.when(core == only)(add)


def correlate_kernel(steps, started, finished, x_ref, high_ref, low_ref, *refs):
    n = len(steps)
    total = refs[n + started]
    if not started:
        total[...] = jnp.zeros_like(total)
    sources = [(ref, far, nears, *(only or [None])) for ref, (far, nears, *only) in zip(refs[:n], steps)]
    add_parts(sources, x_ref, high_ref, low_ref, total, *refs[-2:])
    if finished is not None:
        at_x, _, core = position()
        keep, send = refs[n + started + 1 : n + started + 3]
        for place, block in enumerate(finished):
            keep[place] = total[(at_x + block) % 4, pl.ds(8 * core, 8)]
            send[place] = total[(at_x + block) % 4, pl.ds(8 * (1 - core), 8)]


def correlate(steps, values, tables, total=None, finished=None):
    here = lambda value: pltpu.with_memory_space_constraint(value, pltpu.VMEM)
    started = total is not None
    values = [value.reshape(-1, 2, 4, CH, W) for value in values]
    args = [here(value) for value in (*tables, *values, *([total] if started else []))]
    sums = jax.ShapeDtypeStruct((4, CH, CH, LAGS), jnp.float32)
    half = lambda blocks: jax.ShapeDtypeStruct((len(blocks), 8, CH, LAGS), jnp.float32)
    outs = [sums] + ([half(finished)] * 2 if finished is not None else [])
    pairs = sum(len(step[1]) for step in steps)
    return pl.pallas_call(
        functools.partial(correlate_kernel, steps, started, finished),
        out_shape=outs,
        in_specs=[VMEM] * len(args),
        out_specs=[VMEM] * len(outs),
        scratch_shapes=[pltpu.VMEM((CH * CH, 4 * W), jnp.bfloat16)] * 2,
        input_output_aliases={len(args) - 1: 0} if started else {},
        compiler_params=pltpu.CompilerParams(vmem_limit_bytes=16 * 2**20),
        cost_estimate=pl.CostEstimate(
            flops=6 * CH * CH * 4 * W * LAGS * pairs, bytes_accessed=3 * 2**20 * pairs, transcendentals=0
        ),
    )(*args)


def place_kernel(*refs):
    out_ref = refs[-1]
    at_x, _, core = position()
    for pair, blocks in enumerate(GROUPS):
        mine, other = refs[2 * pair : 2 * pair + 2]
        for place, block in enumerate(blocks):
            out_ref[pl.ds(8 * core, 8), (at_x + block) % 4] = mine[place]
            out_ref[pl.ds(8 * (1 - core), 8), (at_x + block) % 4] = other[place]


def place(pieces):
    return pl.pallas_call(
        place_kernel,
        out_shape=jax.ShapeDtypeStruct((CH, 4, CH, LAGS), jnp.float32),
        in_specs=[VMEM] * len(pieces),
        out_specs=VMEM,
        compiler_params=pltpu.CompilerParams(vmem_limit_bytes=8 * 2**20),
    )(*pieces)


def stage_kernel(high_ref, low_ref, high_out, low_out, sems):
    copies = [
        pltpu.make_async_copy(source, target, sems.at[at])
        for at, (source, target) in enumerate(((high_ref, high_out), (low_ref, low_out)))
    ]
    for copy in copies:
        copy.start()
    for copy in copies:
        copy.wait()


def stage(high, low):
    return pl.pallas_call(
        stage_kernel,
        out_shape=[pltpu.VMEM(high.shape, high.dtype), pltpu.VMEM(low.shape, low.dtype)],
        in_specs=[pl.BlockSpec(memory_space=pl.ANY)] * 2,
        out_specs=[VMEM] * 2,
        scratch_shapes=[pltpu.SemaphoreType.DMA((2,))],
        compiler_params=pltpu.CompilerParams(vmem_limit_bytes=2**20),
    )(high, low)


def shards(spectra):
    me = lax.axis_index("chan")
    at_start, at_near = me % 4 == 0, me // 4 % 2 == 0
    spectra, at_start, at_near = lax.optimization_barrier((spectra, at_start, at_near))
    over_x = lambda c, d: (c + 8 * d) % 32
    over_z = lambda c, d: c // 4 * 4 + (c + d) % 4

    def send(value, d, even, odd):
        pairs = [(w * 32 + c, w * 32 + (odd if w % 2 else even)(c, d)) for w in range(4) for c in range(32)]
        return lax.ppermute(value, ("win", "chan"), pairs)

    other_core = lambda value: lax.ppermute(value, "win", [(w, w ^ 1) for w in range(4)])
    other_chip = lambda value: lax.ppermute(value, "win", [(w, w ^ 2) for w in range(4)])

    high, low = stage(*(jnp.asarray(t) for t in tables()))
    x, *quarters = fold(spectra[0])
    got = [lax.ppermute(quarters[z - 1], "chan", [(8 * s, 8 * s + z) for s in range(4)]) for z in (1, 2, 3)]
    mine = jnp.where(at_start, x[0:2], got[0] + got[1] + got[2])
    mine, high, low = lax.optimization_barrier((mine, high, low))
    over = lax.ppermute(mine, "chan", [(8 * s + z, 8 * s + 4 + z) for s in range(4) for z in range(4)])
    mine = jnp.where(at_near, mine, over)
    swap = lambda at, d: at + d if at % 2 == 0 else at - d
    swap_x = lambda c, d: swap(c // 8, d) % 4 * 8 + c % 8
    swap_z = lambda c, d: c // 4 * 4 + swap(c % 4, d) % 4
    came = {2: send(mine, 2, over_z, over_x)}
    came.update({d: send(mine, d, swap_z, swap_x) for d in (1, -1)})
    first = jnp.stack([came[1], came[-1]])
    second = jnp.stack([mine, came[2]])
    firsts, seconds = {0: first}, {0: second}
    for group, value in ((firsts, first), (seconds, second)):
        for d in (1, -1):
            group[d] = send(value, d, over_x, over_z)
    firsts[2] = send(firsts[1], 1, over_x, over_z)
    seconds[2] = send(seconds[-1], -1, over_x, over_z)

    near, ends = (1, -1), (0, 2)
    tabled = (x, high, low)
    total = correlate([(0, near), (0, ends)], [firsts[0], seconds[0]], tabled)[0]
    total = correlate([(1, near), (-1, ends)], [firsts[1], seconds[-1]], tabled, total)[0]
    total = correlate([(-1, near), (1, ends)], [firsts[-1], seconds[1]], tabled, total)[0]
    values = [firsts[2], seconds[2][0]]
    total, keep, give = correlate([(2, near, 1), (2, (0,), 1)], values, tabled, total, GROUPS[0])
    pair = keep + other_core(give)
    total = correlate([(2, near, 0)], [firsts[2]], tabled, total)[0]
    total, pair = lax.optimization_barrier((total, pair))
    far_pair = other_chip(pair)
    values = [seconds[2][0], seconds[2][1]]
    _, keep, give = correlate([(2, (0,), 0), (2, (2,))], values, tabled, total, GROUPS[1])
    last = keep + other_core(give)
    far_last = other_chip(last)
    far_pair, far_last = lax.optimization_barrier((far_pair, far_last))
    both, both_last = pair + far_pair, last + far_last
    placed = [both, other_core(both), both_last, other_core(both_last)]
    return place(placed).reshape(CH, 4 * CH, LAGS)


def solution(mesh):
    return jax.shard_map(
        shards,
        mesh=mesh,
        in_specs=(P("win", None, "chan", None),),
        out_specs=P("chan", None, None),
        check_vma=False,
    )
```

```python
import functools
import math

import jax
import jax.numpy as jnp
import numpy as np
from jax import lax
from jax.experimental import pallas as pl
from jax.experimental.pallas import tpu as pltpu
from jax.sharding import PartitionSpec as P

LAGS = 256
BINS = 8192
HALF = BINS // 2
CH = 16
WINDOWS = 4
PARTS = 8
W = HALF // PARTS
VMEM = pl.BlockSpec(memory_space=pltpu.VMEM)
GROUPS = ((0, 1, 3), (2,))


def tables():
    lag = np.arange(LAGS) - LAGS // 2
    turns = (np.arange(HALF)[:, None] * lag[None, :]) % BINS
    angle = 2.0 * np.pi * turns / BINS
    cosine, sine = np.cos(angle), -np.sin(angle)
    cosine[0], sine[0] = lag % 2 == 0, lag % 2 != 0
    table = np.concatenate([cosine.reshape(PARTS, W, LAGS), sine.reshape(PARTS, W, LAGS)], axis=1)
    table = table / (math.sqrt(BINS) * WINDOWS)
    high = table.astype(jnp.bfloat16)
    low = (table - high.astype(np.float64)).astype(jnp.bfloat16)
    return high, low


def fold_kernel(x_ref, all_ref, *quarter_refs):
    lane = lax.broadcasted_iota(jnp.int32, (8, 128), 1)
    mirror = lax.rem(128 - lane, 128)
    for part in range(2):
        for rows in (slice(0, 8), slice(8, 16)):
            for tile in range(HALF // 128):
                piece, offset = divmod(tile * 128, W)
                ahead = x_ref[part, rows, tile * 128 : tile * 128 + 128]
                last = BINS - tile * 128
                back = jnp.take_along_axis(x_ref[part, rows, last - 128 : last], mirror, axis=1)
                edge = last if tile else HALF
                back = jnp.where(lane == 0, x_ref[part, rows, edge : edge + 128] if edge < BINS else 0.0, back)
                columns = slice(offset, offset + 128)
                for row, value in ((part, ahead), (2 + part, back)):
                    all_ref[piece, row, rows, columns] = value
                    if piece >= 2:
                        quarter_refs[piece // 2 - 1][piece % 2, row, rows, columns] = value


def fold(x):
    shape = lambda n: jax.ShapeDtypeStruct((n, 4, CH, W), jnp.float32)
    return pl.pallas_call(
        fold_kernel,
        out_shape=[shape(PARTS)] + [shape(2)] * 3,
        in_specs=[VMEM],
        out_specs=[VMEM] * 4,
        compiler_params=pltpu.CompilerParams(vmem_limit_bytes=12 * 2**20),
    )(x)


def position():
    chan = lax.axis_index("chan")
    return chan // 8, chan % 4, lax.axis_index("win") % 2


def add_parts(sources, x_ref, high_ref, low_ref, total, lh, ll):
    at_x, at_z, core = position()
    lane = lax.broadcasted_iota(jnp.int32, (CH, 128), 1)
    dot = functools.partial(jnp.dot, preferred_element_type=jnp.float32)
    for g_ref, far, nears, only in sources:

        def add(g_ref=g_ref, far=far, nears=nears):
            for place, near in enumerate(nears):
                near = jnp.where(jnp.where(core == 0, at_z, at_x) % 2 == 0, -near, near)
                block = (at_x + 4 - jnp.where(core == 0, far, near)) % 4
                bins = (at_z + 4 - jnp.where(core == 0, near, far)) % 4
                first = jnp.logical_and(lane == 0, bins == 0)
                for part in range(2):
                    y = [g_ref[place, part, k] for k in range(4)]
                    for channel in range(CH):
                        x = [x_ref[2 * bins + part, k, channel : channel + 1, :] for k in range(4)]
                        ahead = x[0] * y[0] + x[1] * y[1]
                        back = x[2] * y[2] + x[3] * y[3]
                        even = ahead + back
                        odd = (x[1] * y[0] - x[0] * y[1]) + (x[2] * y[3] - x[3] * y[2])
                        if part == 0:
                            edge = jnp.where(first, ahead[:, :128] - back[:, :128], odd[:, :128])
                            odd = jnp.concatenate([edge, odd[:, 128:]], axis=1)
                        rows = slice(CH * channel, CH * channel + CH)
                        for half, value in enumerate((even, odd)):
                            columns = slice((2 * part + half) * W, (2 * part + half + 1) * W)
                            top = value.astype(jnp.bfloat16)
                            lh[rows, columns] = top
                            ll[rows, columns] = (value - top.astype(jnp.float32)).astype(jnp.bfloat16)
                top = lh[...]
                high = high_ref[pl.ds(2 * bins, 2)].reshape(4 * W, LAGS)
                low = low_ref[pl.ds(2 * bins, 2)].reshape(4 * W, LAGS)
                both = dot(jnp.concatenate([top, ll[...]], axis=0), high)
                got = both[: CH * CH] + both[CH * CH :] + dot(top, low)
                total[block] += got.reshape(CH, CH, LAGS)

        if only is None:
            add()
        else:
            pl.when(core == only)(add)


def correlate_kernel(steps, started, finished, x_ref, high_ref, low_ref, *refs):
    n = len(steps)
    total = refs[n + started]
    if not started:
        total[...] = jnp.zeros_like(total)
    sources = [(ref, far, nears, *(only or [None])) for ref, (far, nears, *only) in zip(refs[:n], steps)]
    add_parts(sources, x_ref, high_ref, low_ref, total, *refs[-2:])
    if finished is not None:
        at_x, _, core = position()
        keep, send = refs[n + started + 1 : n + started + 3]
        for place, block in enumerate(finished):
            keep[place] = total[(at_x + block) % 4, pl.ds(8 * core, 8)]
            send[place] = total[(at_x + block) % 4, pl.ds(8 * (1 - core), 8)]


def correlate(steps, values, tables, total=None, finished=None):
    here = lambda value: pltpu.with_memory_space_constraint(value, pltpu.VMEM)
    started = total is not None
    values = [value.reshape(-1, 2, 4, CH, W) for value in values]
    args = [here(value) for value in (*tables, *values, *([total] if started else []))]
    sums = jax.ShapeDtypeStruct((4, CH, CH, LAGS), jnp.float32)
    half = lambda blocks: jax.ShapeDtypeStruct((len(blocks), 8, CH, LAGS), jnp.float32)
    outs = [sums] + ([half(finished)] * 2 if finished is not None else [])
    pairs = sum(len(step[1]) for step in steps)
    return pl.pallas_call(
        functools.partial(correlate_kernel, steps, started, finished),
        out_shape=outs,
        in_specs=[VMEM] * len(args),
        out_specs=[VMEM] * len(outs),
        scratch_shapes=[pltpu.VMEM((CH * CH, 4 * W), jnp.bfloat16)] * 2,
        input_output_aliases={len(args) - 1: 0} if started else {},
        compiler_params=pltpu.CompilerParams(vmem_limit_bytes=16 * 2**20),
        cost_estimate=pl.CostEstimate(
            flops=6 * CH * CH * 4 * W * LAGS * pairs, bytes_accessed=3 * 2**20 * pairs, transcendentals=0
        ),
    )(*args)


def place_kernel(*refs):
    out_ref, sems = refs[-2:]
    at_x, _, core = position()
    copies = []
    for pair, blocks in enumerate(GROUPS):
        for side, ref in enumerate(refs[2 * pair : 2 * pair + 2]):
            rows = pl.ds(8 * (core if side == 0 else 1 - core), 8)
            for place, block in enumerate(blocks):
                target = out_ref.at[rows, (at_x + block) % 4]
                copies.append(pltpu.make_async_copy(ref.at[place], target, sems.at[len(copies)]))
    for copy in copies:
        copy.start()
    for copy in copies:
        copy.wait()


def place(pieces):
    return pl.pallas_call(
        place_kernel,
        out_shape=jax.ShapeDtypeStruct((CH, 4, CH, LAGS), jnp.float32),
        in_specs=[VMEM] * len(pieces),
        out_specs=pl.BlockSpec(memory_space=pl.ANY),
        scratch_shapes=[pltpu.SemaphoreType.DMA((8,))],
        compiler_params=pltpu.CompilerParams(vmem_limit_bytes=8 * 2**20),
    )(*[pltpu.with_memory_space_constraint(piece, pltpu.VMEM) for piece in pieces])


def stage_kernel(high_ref, low_ref, high_out, low_out, sems):
    copies = [
        pltpu.make_async_copy(source, target, sems.at[at])
        for at, (source, target) in enumerate(((high_ref, high_out), (low_ref, low_out)))
    ]
    for copy in copies:
        copy.start()
    for copy in copies:
        copy.wait()


def stage(high, low):
    return pl.pallas_call(
        stage_kernel,
        out_shape=[pltpu.VMEM(high.shape, high.dtype), pltpu.VMEM(low.shape, low.dtype)],
        in_specs=[pl.BlockSpec(memory_space=pl.ANY)] * 2,
        out_specs=[VMEM] * 2,
        scratch_shapes=[pltpu.SemaphoreType.DMA((2,))],
        compiler_params=pltpu.CompilerParams(vmem_limit_bytes=2**20),
    )(high, low)


def shards(spectra):
    me = lax.axis_index("chan")
    at_start, at_near = me % 4 == 0, me // 4 % 2 == 0
    spectra, at_start, at_near = lax.optimization_barrier((spectra, at_start, at_near))
    over_x = lambda c, d: (c + 8 * d) % 32
    over_z = lambda c, d: c // 4 * 4 + (c + d) % 4

    def send(value, d, even, odd):
        pairs = [(w * 32 + c, w * 32 + (odd if w % 2 else even)(c, d)) for w in range(4) for c in range(32)]
        return lax.ppermute(value, ("win", "chan"), pairs)

    other_core = lambda value: lax.ppermute(value, "win", [(w, w ^ 1) for w in range(4)])
    other_chip = lambda value: lax.ppermute(value, "win", [(w, w ^ 2) for w in range(4)])

    high, low = stage(*(jnp.asarray(t) for t in tables()))
    x, *quarters = fold(spectra[0])
    got = [lax.ppermute(quarters[z - 1], "chan", [(8 * s, 8 * s + z) for s in range(4)]) for z in (1, 2, 3)]
    mine = jnp.where(at_start, x[0:2], got[0] + got[1] + got[2])
    mine, high, low = lax.optimization_barrier((mine, high, low))
    over = lax.ppermute(mine, "chan", [(8 * s + z, 8 * s + 4 + z) for s in range(4) for z in range(4)])
    mine = jnp.where(at_near, mine, over)
    swap = lambda at, d: at + d if at % 2 == 0 else at - d
    swap_x = lambda c, d: swap(c // 8, d) % 4 * 8 + c % 8
    swap_z = lambda c, d: c // 4 * 4 + swap(c % 4, d) % 4
    came = {2: send(mine, 2, over_z, over_x)}
    came.update({d: send(mine, d, swap_z, swap_x) for d in (1, -1)})
    first = jnp.stack([came[1], came[-1]])
    second = jnp.stack([mine, came[2]])
    firsts, seconds = {0: first}, {0: second}
    for group, value in ((firsts, first), (seconds, second)):
        for d in (1, -1):
            group[d] = send(value, d, over_x, over_z)
    firsts[2] = send(firsts[1], 1, over_x, over_z)
    seconds[2] = send(seconds[-1], -1, over_x, over_z)

    near, ends = (1, -1), (0, 2)
    tabled = (x, high, low)
    total = correlate([(0, near), (0, ends)], [firsts[0], seconds[0]], tabled)[0]
    total = correlate([(1, near), (-1, ends)], [firsts[1], seconds[-1]], tabled, total)[0]
    total = correlate([(-1, near), (1, ends)], [firsts[-1], seconds[1]], tabled, total)[0]
    values = [firsts[2], seconds[2][0]]
    total, keep, give = correlate([(2, near, 1), (2, (0,), 1)], values, tabled, total, GROUPS[0])
    pair = keep + other_core(give)
    total = correlate([(2, near, 0)], [firsts[2]], tabled, total)[0]
    total, pair = lax.optimization_barrier((total, pair))
    far_pair = other_chip(pair)
    values = [seconds[2][0], seconds[2][1]]
    _, keep, give = correlate([(2, (0,), 0), (2, (2,))], values, tabled, total, GROUPS[1])
    last = keep + other_core(give)
    far_last = other_chip(last)
    far_pair, far_last = lax.optimization_barrier((far_pair, far_last))
    both, both_last = pair + far_pair, last + far_last
    placed = [both, other_core(both), both_last, other_core(both_last)]
    return place(placed).reshape(CH, 4 * CH, LAGS)


def solution(mesh):
    return jax.shard_map(
        shards,
        mesh=mesh,
        in_specs=(P("win", None, "chan", None),),
        out_specs=P("chan", None, None),
        check_vma=False,
    )
```
